512 devices in a mesh: clus: 128 (over z, x, core), sk: 4 (over y).
Axes of the slice: x: 4, y: 4, z: 16, core: 2. Of those that a mesh axis runs over, the one named last changes fastest.
Arguments:
- positions: float32 [3, 1048576], P(None, 'clus'), as said below
- sketch: bfloat16 [256, 1048576], P('sk', 'clus'), may hold values from -24 to 24
- near: int32 [4096, 9], P('clus'), may hold values from 0 to 1, as said below
Outputs:
- sketch_image: float32 [256, 1048576], P('sk', 'clus')
- node_factor: float32 [32768, 256], P('clus', 'sk')
- pair_factor: float32 [32768, 256], P('clus', 'sk')
- group_factor: float32 [32768, 256], P('clus', 'sk')
The draws below stay inside these ranges and needn't reach their ends.
Inputs may be any that keep to these rules, and one draw needn't show every extreme that they name: `positions`: column i is the position of point i, which belongs to cluster i // 256. Along the first coordinate each cluster occupies an interval of its own; these intervals do not intersect, and a cluster with a larger index lies entirely at larger first coordinates than one with a smaller index. The second and third coordinates lie in [0, 1). near[c, 4 + d] is 1 where cluster c + d exists and lies in the near field of cluster c, else 0; columns 3, 4 and 5 are 1 wherever that cluster exists; the relation is symmetric: near[c, 4 + d] = near[c + d, 4 - d].
All inputs are finite; a program needn't handle non-finite values.
Results may differ from the reference program's by a relative error of at most 0.00057.
Values may be sent and summed in bfloat16 or wider, within the bound.
No kernel may reach another device: no remote copies, remote signals or barrier semaphores. Data moves between devices by JAX's collectives and lax.ppermute only.
A program may use at most 128 MiB of HBM per device.

```python
import math
import jax
import jax.numpy as jnp
from jax import lax

CS = 256
R = 256
H = 4
ROWS = 8192
CLUSTERS = 4096
NPTS = 1048576
N_CLUS = 128


def cluster_widths(key):
    return jax.random.randint(key, (CLUSTERS,), 1, 5).astype(jnp.int32)


def cluster_bounds(widths):
    return jnp.concatenate([jnp.zeros((1,), jnp.int32), jnp.cumsum(widths).astype(jnp.int32)])


def draw_near(key, part):
    widths = cluster_widths(key)
    bounds = cluster_bounds(widths)
    cluster_ids = jnp.arange(CLUSTERS, dtype=jnp.int32)
    columns = []
    for shift_by in range(-H, H + 1):
        other = cluster_ids + shift_by
        if shift_by == 0:
            flags = jnp.ones((CLUSTERS,), jnp.int32)
        elif shift_by > 0:
            inside = other < CLUSTERS
            between = bounds[jnp.minimum(other, CLUSTERS)] - bounds[cluster_ids + 1]
            flags = (inside & (between < 4)).astype(jnp.int32)
        else:
            inside = other >= 0
            between = bounds[cluster_ids] - bounds[jnp.maximum(other + 1, 0)]
            flags = (inside & (between < 4)).astype(jnp.int32)
        columns.append(flags)
    return jnp.stack(columns, axis=1)


def draw_positions(key, part):
    widths = cluster_widths(key)
    key = jax.random.fold_in(key, 23)
    bounds = cluster_bounds(widths)
    first_key, second_key, third_key = jax.random.split(key, 3)
    along_first = jax.random.uniform(first_key, (NPTS,), jnp.float32)
    along_second = jax.random.uniform(second_key, (NPTS,), jnp.float32)
    along_third = jax.random.uniform(third_key, (NPTS,), jnp.float32)
    owner_ids = jnp.arange(NPTS, dtype=jnp.int32) // CS
    begin = bounds[owner_ids].astype(jnp.float32)
    extent = widths[owner_ids].astype(jnp.float32)
    first = (begin + extent * along_first) * 0.25
    return jnp.stack([first, along_second, along_third]).astype(jnp.float32)


def spiked(drawn, rng, source, target, shards_of, factor):
    owner, partner = [(jnp.arange(drawn.shape[dim]) // (drawn.shape[dim] // shards_of)).reshape([-1 if axis == dim else 1 for axis in range(drawn.ndim)]) for dim in (source, target)]
    chosen = jax.random.permutation(rng, shards_of)[partner]
    strong = (owner == chosen) | (owner == (partner + shards_of // 2) % shards_of)
    return jnp.where(strong, factor * drawn, drawn)


def block_levels(own_key, shape, cuts, low, largest):
    level, own = 1.0, jax.random.fold_in(own_key, 6)
    for dim, parts in cuts:
        steps = jnp.exp(jax.random.uniform(jax.random.fold_in(own, dim), (parts,), jnp.float32, low / len(cuts), largest / len(cuts)))
        level = level * jnp.repeat(steps, shape[dim] // parts).reshape([-1 if axis == dim else 1 for axis in range(len(shape))])
    return level


def noise_with(own_key, shape, deviation, reach, shards, heavy, held_as=jnp.bfloat16):
    array = deviation * jax.random.normal(own_key, shape, jnp.float32)
    if shards:
        array = array * block_levels(own_key, shape, shards, -0.22, 0.18)
    return jnp.clip(spiked(array, jax.random.fold_in(own_key, 3), *heavy), -reach, reach).astype(held_as)


def setup_inputs(seed: int = 0) -> dict:
    keys = jax.random.split(jax.random.key(seed), 4)
    return {
        "positions": draw_positions(jax.random.fold_in(keys[3], 71), 0),
        "sketch": noise_with(keys[1], (R, NPTS), 1.0, 24.0, ((0, 4), (1, 128)), (1, 0, 128, 5.5)),
        "near": draw_near(jax.random.fold_in(keys[3], 71), 0),
    }


decay_rate = math.sqrt(3.0) / 0.3
nugget = 1.0

def kernel_tile(sources, targets):
    squared = (sources[0][:, None] - targets[0][None, :]) * (sources[0][:, None] - targets[0][None, :])
    squared = squared + (sources[1][:, None] - targets[1][None, :]) * (sources[1][:, None] - targets[1][None, :])
    squared = squared + (sources[2][:, None] - targets[2][None, :]) * (sources[2][:, None] - targets[2][None, :])
    scaled = decay_rate * jnp.sqrt(squared)
    return (1.0 + scaled) * jnp.exp(-scaled)

def reference(positions, sketch, near):
    margin = H * CS
    window = (2 * H + 1) * CS
    kernel_scale = 8.0 / CS
    pad_positions = jnp.pad(positions, ((0, 0), (margin, margin)))
    pad_sketch = jnp.pad(sketch, ((0, 0), (margin, margin)))

    def one_cluster(index):
        begin = (index * CS).astype(jnp.int32)
        sources = lax.dynamic_slice_in_dim(pad_positions, begin, window, 1)
        targets = lax.dynamic_slice_in_dim(positions, begin, CS, 1)
        sketch_win = lax.dynamic_slice_in_dim(pad_sketch, begin, window, 1)
        own_cols = lax.dynamic_slice_in_dim(sketch, begin, CS, 1)
        near_mask = jnp.repeat(near[index].astype(jnp.float32), CS)
        tile = (kernel_tile(sources, targets) * near_mask[:, None]).astype(jnp.bfloat16)
        product = jnp.dot(sketch_win.astype(jnp.float32), tile.astype(jnp.float32), preferred_element_type=jnp.float32)
        return kernel_scale * product + nugget * own_cols.astype(jnp.float32)
    blocks = lax.map(one_cluster, jnp.arange(CLUSTERS, dtype=jnp.int32))
    sketch_image = jnp.transpose(blocks, (1, 0, 2)).reshape(R, NPTS)
    rounded = sketch_image.astype(jnp.bfloat16)

    def node_gram(index):
        columns = lax.dynamic_slice_in_dim(rounded, (index * ROWS).astype(jnp.int32), ROWS, 1)
        product = lax.dot_general(columns.astype(jnp.float32), columns.astype(jnp.float32), (((1,), (1,)), ((), ())), preferred_element_type=jnp.float32)
        return product / ROWS
    gram_node = lax.map(node_gram, jnp.arange(N_CLUS, dtype=jnp.int32))
    paired = gram_node.reshape(N_CLUS // 2, 2, R, R)
    pair_unique = (paired[:, 0] + paired[:, 1]) * 0.5
    gram_pair = jnp.repeat(pair_unique, 2, axis=0)
    grouped = pair_unique.reshape(N_CLUS // 4, 2, R, R)
    group_unique = (grouped[:, 0] + grouped[:, 1]) * 0.5
    gram_group = jnp.repeat(group_unique, 4, axis=0)
    node_factor = jnp.linalg.cholesky(gram_node).reshape(N_CLUS * R, R)
    pair_factor = jnp.linalg.cholesky(gram_pair).reshape(N_CLUS * R, R)
    group_factor = jnp.linalg.cholesky(gram_group).reshape(N_CLUS * R, R)
    return (sketch_image, node_factor, pair_factor, group_factor)
```

```python
import math

import jax
import jax.numpy as jnp
from jax import lax
from jax.experimental import pallas as pl
from jax.experimental.pallas import tpu as pltpu
from jax.sharding import Mesh
from jax.sharding import PartitionSpec as P

CS = 256
H = 4
MIB = 2**20
RATE = math.sqrt(3.0) / 0.3
NUGGET = 1.0
FAMILY = 4
UNROLL = 4
PANEL = 16
SHIFT = 64


def near_field_kernel(pos, sk, low, high, near, image, rounded, across, along, cols, acc, todo):
    slices, rows = sk.shape
    own = rows // CS
    last = own + 2 * H

    def joined(block):
        parts = [block[slices + r : slices + r + 1, :].astype(jnp.float32) for r in range(9)]
        return jnp.concatenate([parts[r] + parts[r + 1] + parts[r + 2] for r in (0, 3, 6)], axis=0)

    for slot in range(last):
        if slot < H:
            a = slot * CS
            block, p = low[:slices, a : a + CS], joined(low[:, a : a + CS])
        elif slot < H + own:
            a = (slot - H) * CS
            block, p = sk[:, a : a + CS], pos[:, a : a + CS]
        else:
            a = (slot - H - own) * CS
            block, p = high[:slices, a : a + CS], joined(high[:, a : a + CS])
        cols[slot] = block
        for r in range(3):
            along[slot, :, r * 128 : (r + 1) * 128] = jnp.broadcast_to(p[r : r + 1, :], (128, CS)).T
        across[slot] = p
        acc[slot] = jnp.zeros((slices, CS), jnp.float32)
    cols[last] = jnp.zeros((slices, CS), jnp.bfloat16)
    along[last] = jnp.zeros((CS, 384), jnp.float32)
    across[last] = jnp.zeros((3, CS), jnp.float32)

    def tile(c, s):
        squared = 1e-30
        for r in range(3):
            point = along[s, :, r * 128 : (r + 1) * 128]
            diff = jnp.concatenate([point, point], axis=1) - across[c, r : r + 1]
            squared = squared + diff * diff
        dist = squared * lax.rsqrt(squared)
        return ((1.0 + RATE * dist) * jnp.exp2(dist * (-RATE * math.log2(math.e)))).astype(jnp.bfloat16)

    def forward(s, t):
        return jnp.dot(cols[s], t, preferred_element_type=jnp.float32)

    def backward(c, t):
        return lax.dot_general(cols[c], t, (((1,), (1,)), ((), ())), preferred_element_type=jnp.float32)

    count = jnp.int32(0)
    for s in range(H):
        for d in range(s + 1, H + 1):
            todo[count] = (s - d + H) * SHIFT + s + H
            count = count + near[s, H - d]

    def close_step(i, count):
        results = []
        for u in range(2):
            c = i * 2 + u
            for d in range(2, H + 1):
                todo[count] = (c + H) * SHIFT + c + d + H
                count = count + near[c, H + d]
            c = c + H
            same, next_one = tile(c, c), tile(c, c + 1)
            results.append((c, forward(c, same) + forward(c + 1, next_one), backward(c, next_one)))
        for c, here, there in results:
            acc[c] = acc[c] + here
            acc[c + 1] = acc[c + 1] + there
        return count

    count = lax.fori_loop(0, own // 2, close_step, count)
    for i in range(UNROLL):
        todo[count + i] = last * (SHIFT + 1)

    def far_step(i, carry):
        results = []
        for u in range(UNROLL):
            code = todo[i * UNROLL + u]
            c, s = code // SHIFT, code % SHIFT
            t = tile(c, s)
            results.append((c, s, forward(s, t), backward(c, t)))
        for c, s, here, there in results:
            acc[c] = acc[c] + here
            acc[s] = acc[s] + there
        return carry

    lax.fori_loop(0, (count + UNROLL - 1) // UNROLL, far_step, 0)

    per = own // rounded.shape[0]
    for c in range(own):
        value = acc[c + H] * (8.0 / CS) + NUGGET * cols[c + H].astype(jnp.float32)
        image[:, c * CS : (c + 1) * CS] = value
        rounded[c // per, :, (c % per) * CS : (c % per + 1) * CS] = value.astype(jnp.bfloat16)


def near_field(pos, sk, low, high, near, shares):
    slices, rows = sk.shape
    slots = rows // CS + 2 * H + 1
    whole = pl.BlockSpec(memory_space=pltpu.VMEM)
    return pl.pallas_call(
        near_field_kernel,
        out_shape=(
            jax.ShapeDtypeStruct((slices, rows), jnp.float32),
            jax.ShapeDtypeStruct((shares, slices, rows // shares), jnp.bfloat16),
        ),
        in_specs=[whole, whole, whole, whole, pl.BlockSpec(memory_space=pltpu.SMEM)],
        out_specs=(whole, whole),
        scratch_shapes=[
            pltpu.VMEM((slots, 3, CS), jnp.float32),
            pltpu.VMEM((slots, CS, 3 * 128), jnp.float32),
            pltpu.VMEM((slots, slices, CS), jnp.bfloat16),
            pltpu.VMEM((slots, slices, CS), jnp.float32),
            pltpu.SMEM((slots * H + 2 * UNROLL,), jnp.int32),
        ],
        compiler_params=pltpu.CompilerParams(vmem_limit_bytes=36 * MIB),
        name="near_field",
    )(pos, sk, low, high, near)


def gram_kernel(points, out, *, scale):
    whole = points[...].reshape(-1, points.shape[-1])
    half = whole.shape[0] // 2
    product = lax.dot_general(whole, whole, (((1,), (1,)), ((), ())), preferred_element_type=jnp.float32) * scale
    out[:half] = product[:half, :half]
    out[half : 2 * half] = product[:half, half:]
    out[2 * half :] = product[half:, half:]


def partial_gram(points, scale):
    half = points.shape[0] * points.shape[1] // 2
    return pl.pallas_call(
        lambda points, out: gram_kernel(points, out, scale=scale),
        out_shape=jax.ShapeDtypeStruct((3 * half, half), jnp.float32),
        compiler_params=pltpu.CompilerParams(vmem_limit_bytes=32 * MIB),
        name="partial_gram",
    )(points)


def combine_kernel(parts, out):
    k, s = out.shape[0], out.shape[1]
    nodes = []
    for i in range(k):
        total = parts[i * s]
        for j in range(1, s):
            total = total + parts[i * s + j]
        nodes.append(total)
    pairs = [(nodes[i] + nodes[i + 1]) * 0.5 for i in range(0, k, 2)]
    group = (pairs[0] + pairs[1]) * 0.5
    for i in range(k):
        for j in range(s):
            out[i, j, 0] = nodes[i]
            out[i, j, 1] = pairs[i // 2]
            out[i, j, 2] = group


def combine(parts, k, s):
    return pl.pallas_call(
        combine_kernel,
        out_shape=jax.ShapeDtypeStruct((k, s, 3) + parts.shape[1:], jnp.float32),
        name="combine",
    )(parts)


def pieces(value):
    high = value.astype(jnp.bfloat16)
    rest = value - high.astype(jnp.float32)
    mid = rest.astype(jnp.bfloat16)
    low = (rest - mid.astype(jnp.float32)).astype(jnp.bfloat16)
    return high, mid, low


def cholesky_kernel(place, slabs, first, second, third, work, upper):
    sources, mats, depth, half = slabs.shape
    n = 2 * half
    for j in range(sources):
        for t in range(0, depth, 8):
            row = j * depth + t
            block, at = row // half, row % half
            for m in range(mats):
                value = slabs[j, m, t : t + 8]
                if block < 2:
                    work[m, at : at + 8, block * half : (block + 1) * half] = value
                else:
                    work[m, half + at : half + at + 8, half:] = value
    for m in range(mats):
        upper[m, half:, :half] = jnp.zeros((half, half), jnp.float32)
    rowid = lax.broadcasted_iota(jnp.int32, (8, 128), 0)
    spread = lambda row: jnp.broadcast_to(row, (8, 128))
    for j0 in range(0, n, PANEL):
        lane0 = 0 if j0 < half else half
        width = (n - lane0) // 128
        rows, cols, scale = [], [], []
        for m in range(mats):
            block = work[m, j0 : j0 + PANEL, lane0:]
            rows.append(
                [[block[8 * h : 8 * h + 8, 128 * w : 128 * w + 128] for w in range(width)] for h in range(2)]
            )
            at = j0 - lane0
            cols.append(
                [[spread(block[8 * h : 8 * h + 8, at + c : at + c + 1]) for h in range(2)] for c in range(PANEL)]
            )
            scale.append([jnp.zeros((8, 128), jnp.float32) for h in range(2)])
        for q in range(PANEL):
            hq, r = q // 8, q % 8
            for m in range(mats):
                inv = lax.rsqrt(spread(cols[m][q][hq][r : r + 1, :]))
                scale[m][hq] = jnp.where(rowid == r, inv, scale[m][hq])
                inv2 = inv * inv
                factor = [None, None]
                for h in range(hq, 2):
                    f = cols[m][q][h] * inv2
                    factor[h] = jnp.where(rowid > r, f, 0.0) if h == hq else f
                for c in range(q + 1, PANEL):
                    row = spread(cols[m][c][hq][r : r + 1, :])
                    for h in range(hq, 2):
                        cols[m][c][h] = cols[m][c][h] - factor[h] * row
                for w in range(width):
                    row = spread(rows[m][hq][w][r : r + 1, :])
                    for h in range(hq, 2):
                        rows[m][h][w] = rows[m][h][w] - factor[h] * row
        for m in range(mats):
            done = jnp.concatenate(
                [
                    jnp.concatenate([rows[m][h][w] * scale[m][h] for w in range(width)], axis=1)
                    for h in range(2)
                ],
                axis=0,
            )
            upper[m, j0 : j0 + PANEL, lane0:] = done
            start = j0 + PANEL
            if start < n:
                high, mid, low = pieces(done)
                skip = (0 if start < half else half) - lane0
                left = jnp.concatenate([high, high, mid, high, mid, low], axis=0)[:, skip:]
                right = jnp.concatenate([high, mid, high, low, mid, high], axis=0)[:, skip:]
                product = lax.dot_general(left, right, (((0,), (0,)), ((), ())), preferred_element_type=jnp.float32)
                if start < half:
                    work[m, start:half, :] = work[m, start:half, :] - product[start:half, :]
                    work[m, half:, half:] = work[m, half:, half:] - product[half:, half:]
                else:
                    work[m, start:, half:] = work[m, start:, half:] - product[start - half :, :]
    wide = first.shape[1]
    begin = pl.multiple_of(place[0] * wide, wide)
    i = lax.broadcasted_iota(jnp.int32, (wide, n), 0) + begin
    j = lax.broadcasted_iota(jnp.int32, (wide, n), 1)
    for m, out in enumerate((first, second, third)):
        out[...] = jnp.where(j >= i, upper[m, pl.ds(begin, wide), :], 0.0).T


def cholesky(place, slabs, wide):
    half = slabs.shape[3]
    whole = pl.BlockSpec(memory_space=pltpu.VMEM)
    return pl.pallas_call(
        cholesky_kernel,
        out_shape=(jax.ShapeDtypeStruct((2 * half, wide), jnp.float32),) * 3,
        in_specs=[pl.BlockSpec(memory_space=pltpu.SMEM), whole],
        out_specs=(whole,) * 3,
        scratch_shapes=[pltpu.VMEM((3, 2 * half, 2 * half), jnp.float32)] * 2,
        compiler_params=pltpu.CompilerParams(vmem_limit_bytes=32 * MIB),
        name="cholesky",
    )(place, slabs)


def edge(positions, sketch):
    high = lax.reduce_precision(positions, 8, 7)
    rest = positions - high
    mid = lax.reduce_precision(rest, 8, 7)
    parts = jnp.stack([high, mid, rest - mid], axis=1).reshape(9, -1).astype(jnp.bfloat16)
    return jnp.concatenate([sketch, jnp.pad(parts, ((0, 7), (0, 0)))], axis=0)


def on_device(positions, sketch, near):
    slices, rows = sketch.shape
    margin = H * CS
    clus = ("tree", "child")
    count = lax.axis_size(clus)
    shares = lax.axis_size("sk")
    forward = [(i, i + 1) for i in range(count - 1)]
    backward = [(i + 1, i) for i in range(count - 1)]
    low = lax.ppermute(edge(positions[:, -margin:], sketch[:, -margin:]), clus, forward)
    high = lax.ppermute(edge(positions[:, :margin], sketch[:, :margin]), clus, backward)
    image, rounded = near_field(positions, sketch, low, high, near, shares)
    traded = lax.all_to_all(rounded, "sk", split_axis=0, concat_axis=0, tiled=True)
    gram = partial_gram(traded, 1.0 / rows)
    family = FAMILY * shares
    slab = gram.reshape(family, -1, gram.shape[1])
    parts = lax.all_to_all(slab, ("child", "sk"), split_axis=0, concat_axis=0, tiled=True)
    sums = combine(parts, FAMILY, shares)
    sums = sums.reshape(family, 3 * slab.shape[1], slab.shape[2])
    slabs = lax.all_to_all(sums, ("child", "sk"), split_axis=0, concat_axis=0, tiled=True)
    slabs = slabs.reshape(family, 3, slab.shape[1], slab.shape[2])
    place = lax.axis_index("sk").astype(jnp.int32).reshape(1)
    return (image, *cholesky(place, slabs, slices))


def solution(mesh):
    clusters, shares = mesh.devices.shape
    split = Mesh(mesh.devices.reshape(clusters // FAMILY, FAMILY, shares), ("tree", "child", "sk"))
    clus = ("tree", "child")
    return jax.shard_map(
        on_device,
        mesh=split,
        in_specs=(P(None, clus), P("sk", clus), P(clus, None)),
        out_specs=(P("sk", clus), P(clus, "sk"), P(clus, "sk"), P(clus, "sk")),
        check_vma=False,
    )
```

```python
import math

import jax
import jax.numpy as jnp
from jax import lax
from jax.experimental import pallas as pl
from jax.experimental.pallas import tpu as pltpu
from jax.sharding import Mesh
from jax.sharding import PartitionSpec as P

CS = 256
H = 4
MIB = 2**20
RATE = math.sqrt(3.0) / 0.3
NUGGET = 1.0
FAMILY = 4
UNROLL = 4
PANEL = 16
SHIFT = 64


def near_field_kernel(pos, sk, low, high, near, image, rounded, across, along, cols, acc, held, todo):
    slices, rows = sk.shape
    own = rows // CS
    half = CS // 2
    last = own + 2 * H

    def joined(block):
        parts = [block[slices + r : slices + r + 1, :].astype(jnp.float32) for r in range(9)]
        return jnp.concatenate([parts[r] + parts[r + 1] + parts[r + 2] for r in (0, 3, 6)], axis=0)

    def copy_along(slot):
        for r in range(3):
            along[slot, :, r * 128 : (r + 1) * 128] = jnp.broadcast_to(across[slot, r : r + 1], (128, CS)).T

    for slot in range(last):
        if slot < H:
            a = slot * CS
            block, p = low[:slices, a : a + CS], joined(low[:, a : a + CS])
        elif slot < H + own:
            a = (slot - H) * CS
            block, p = sk[:, a : a + CS], pos[:, a : a + CS]
        else:
            a = (slot - H - own) * CS
            block, p = high[:slices, a : a + CS], joined(high[:, a : a + CS])
        cols[slot] = block
        across[slot] = p
        acc[slot] = jnp.zeros((slices, CS), jnp.float32)
    cols[last] = jnp.zeros((slices, CS), jnp.bfloat16)
    along[last] = jnp.zeros((CS, 384), jnp.float32)
    across[last] = jnp.zeros((3, CS), jnp.float32)
    for slot in range(H, H + 3):
        copy_along(slot)
    for slot in range(H + own, last):
        copy_along(slot)

    def tile(c, s, i=0, j=0, size=CS):
        squared = 1e-30
        for r in range(3):
            point = along[s, i : i + size, r * 128 : (r + 1) * 128]
            if size > 128:
                point = jnp.concatenate([point, point], axis=1)
            diff = point - across[c, r : r + 1, j : j + size]
            squared = squared + diff * diff
        dist = squared * lax.rsqrt(squared)
        return ((1.0 + RATE * dist) * jnp.exp2(dist * (-RATE * math.log2(math.e)))).astype(jnp.bfloat16)

    def product(x, t):
        return jnp.dot(x, t, preferred_element_type=jnp.float32)

    def product_t(x, t):
        return lax.dot_general(x, t, (((1,), (1,)), ((), ())), preferred_element_type=jnp.float32)

    count = jnp.int32(UNROLL)
    for s in range(H):
        for d in range(s + 1, H + 1):
            todo[count] = (s - d + H) * SHIFT + s + H
            count = count + near[H - d, s]

    def close_products(c, buf):
        x = cols[c]
        t = held[buf + 1]
        ahead = product(cols[c + 1], t)
        acc[c] = acc[c] + (product(x, held[buf]) + ahead)
        acc[c + 1] = acc[c + 1] + product_t(x, t)

    def close_tiles(c, buf):
        held[buf, :half, :half] = tile(c, c, 0, 0, half)
        corner = tile(c, c, 0, half, half)
        held[buf, :half, half:] = corner
        held[buf, half:, :half] = corner.T
        held[buf, half:, half:] = tile(c, c, half, half, half)
        held[buf + 1] = tile(c, c + 1)

    def close_step(i, count):
        c = i * 2 + H
        for u in range(2):
            close_products(c - 2 + u, 2 * u)
        for u in range(2):
            for d in range(2, H + 1):
                todo[count] = (c + u) * SHIFT + c + u + d
                count = count + near[H + d, c + u - H]
            copy_along(c + u + 3)
            close_tiles(c + u, 2 * u)
        return count

    held[...] = jnp.zeros(held.shape, jnp.bfloat16)
    count = lax.fori_loop(0, own // 2, close_step, count)
    for u in range(2):
        close_products(H + own - 2 + u, 2 * u)
    for slot in range(H):
        copy_along(slot)
    for i in range(UNROLL):
        todo[i] = last * (SHIFT + 1)
        todo[count + i] = last * (SHIFT + 1)

    def far_products(i):
        for u in range(UNROLL):
            code = todo[i * UNROLL + u]
            c, s = code // SHIFT, code % SHIFT
            t = held[u]
            acc[c] = acc[c] + product(cols[s], t)
            acc[s] = acc[s] + product_t(cols[c], t)

    def far_step(i, carry):
        far_products(i - 1)
        for u in range(UNROLL):
            code = todo[i * UNROLL + u]
            held[u] = tile(code // SHIFT, code % SHIFT)
        return carry

    steps = (count + UNROLL - 1) // UNROLL
    lax.fori_loop(1, steps, far_step, 0)
    far_products(steps - 1)

    per = own // rounded.shape[0]
    for c in range(own):
        value = acc[c + H] * (8.0 / CS) + NUGGET * cols[c + H].astype(jnp.float32)
        image[:, c * CS : (c + 1) * CS] = value
        rounded[c // per, :, (c % per) * CS : (c % per + 1) * CS] = value.astype(jnp.bfloat16)


def near_field(pos, sk, low, high, near, shares):
    slices, rows = sk.shape
    slots = rows // CS + 2 * H + 1
    whole = pl.BlockSpec(memory_space=pltpu.VMEM)
    return pl.pallas_call(
        near_field_kernel,
        out_shape=(
            jax.ShapeDtypeStruct((slices, rows), jnp.float32),
            jax.ShapeDtypeStruct((shares, slices, rows // shares), jnp.bfloat16),
        ),
        in_specs=[whole, whole, whole, whole, pl.BlockSpec(memory_space=pltpu.SMEM)],
        out_specs=(whole, whole),
        scratch_shapes=[
            pltpu.VMEM((slots, 3, CS), jnp.float32),
            pltpu.VMEM((slots, CS, 3 * 128), jnp.float32),
            pltpu.VMEM((slots, slices, CS), jnp.bfloat16),
            pltpu.VMEM((slots, slices, CS), jnp.float32),
            pltpu.VMEM((UNROLL, CS, CS), jnp.bfloat16),
            pltpu.SMEM((slots * H + 4 * UNROLL,), jnp.int32),
        ],
        compiler_params=pltpu.CompilerParams(vmem_limit_bytes=36 * MIB),
        name="near_field",
    )(pos, sk, low, high, near)


def gram_kernel(points, out, *, scale):
    whole = points[...].reshape(-1, points.shape[-1])
    half = whole.shape[0] // 2
    product = lax.dot_general(whole, whole, (((1,), (1,)), ((), ())), preferred_element_type=jnp.float32) * scale
    out[:half] = product[:half, :half]
    out[half : 2 * half] = product[:half, half:]
    out[2 * half :] = product[half:, half:]


def partial_gram(points, scale):
    half = points.shape[0] * points.shape[1] // 2
    return pl.pallas_call(
        lambda points, out: gram_kernel(points, out, scale=scale),
        out_shape=jax.ShapeDtypeStruct((3 * half, half), jnp.float32),
        compiler_params=pltpu.CompilerParams(vmem_limit_bytes=32 * MIB),
        name="partial_gram",
    )(points)


def combine_kernel(parts, out):
    k, s = out.shape[0], out.shape[1]
    nodes = []
    for i in range(k):
        total = parts[i * s]
        for j in range(1, s):
            total = total + parts[i * s + j]
        nodes.append(total)
    pairs = [(nodes[i] + nodes[i + 1]) * 0.5 for i in range(0, k, 2)]
    group = (pairs[0] + pairs[1]) * 0.5
    for i in range(k):
        for j in range(s):
            out[i, j, 0] = nodes[i]
            out[i, j, 1] = pairs[i // 2]
            out[i, j, 2] = group


def combine(parts, k, s):
    return pl.pallas_call(
        combine_kernel,
        out_shape=jax.ShapeDtypeStruct((k, s, 3) + parts.shape[1:], jnp.float32),
        name="combine",
    )(parts)


def pieces(value):
    high = value.astype(jnp.bfloat16)
    rest = value - high.astype(jnp.float32)
    mid = rest.astype(jnp.bfloat16)
    low = (rest - mid.astype(jnp.float32)).astype(jnp.bfloat16)
    return high, mid, low


def cholesky_kernel(place, slabs, first, second, third, work, upper):
    sources, mats, depth, half = slabs.shape
    n = 2 * half
    for j in range(sources):
        for t in range(0, depth, 8):
            row = j * depth + t
            block, at = row // half, row % half
            for m in range(mats):
                value = slabs[j, m, t : t + 8]
                if block < 2:
                    work[m, at : at + 8, block * half : (block + 1) * half] = value
                else:
                    work[m, half + at : half + at + 8, half:] = value
    for m in range(mats):
        upper[m, half:, :half] = jnp.zeros((half, half), jnp.float32)
    rowid = lax.broadcasted_iota(jnp.int32, (8, 128), 0)
    spread = lambda row: jnp.broadcast_to(row, (8, 128))
    for j0 in range(0, n, PANEL):
        lane0 = 0 if j0 < half else half
        width = (n - lane0) // 128
        rows, cols, scale = [], [], []
        for m in range(mats):
            block = work[m, j0 : j0 + PANEL, lane0:]
            rows.append(
                [[block[8 * h : 8 * h + 8, 128 * w : 128 * w + 128] for w in range(width)] for h in range(2)]
            )
            at = j0 - lane0
            cols.append(
                [[spread(block[8 * h : 8 * h + 8, at + c : at + c + 1]) for h in range(2)] for c in range(PANEL)]
            )
            scale.append([jnp.zeros((8, 128), jnp.float32) for h in range(2)])
        for q in range(PANEL):
            hq, r = q // 8, q % 8
            for m in range(mats):
                inv = lax.rsqrt(spread(cols[m][q][hq][r : r + 1, :]))
                scale[m][hq] = jnp.where(rowid == r, inv, scale[m][hq])
                inv2 = inv * inv
                factor = [None, None]
                for h in range(hq, 2):
                    f = cols[m][q][h] * inv2
                    factor[h] = jnp.where(rowid > r, f, 0.0) if h == hq else f
                for c in range(q + 1, PANEL):
                    row = spread(cols[m][c][hq][r : r + 1, :])
                    for h in range(hq, 2):
                        cols[m][c][h] = cols[m][c][h] - factor[h] * row
                for w in range(width):
                    row = spread(rows[m][hq][w][r : r + 1, :])
                    for h in range(hq, 2):
                        rows[m][h][w] = rows[m][h][w] - factor[h] * row
        for m in range(mats):
            done = jnp.concatenate(
                [
                    jnp.concatenate([rows[m][h][w] * scale[m][h] for w in range(width)], axis=1)
                    for h in range(2)
                ],
                axis=0,
            )
            upper[m, j0 : j0 + PANEL, lane0:] = done
            start = j0 + PANEL
            if start < n:
                high, mid, low = pieces(done)
                skip = (0 if start < half else half) - lane0
                left = jnp.concatenate([high, high, mid, high, mid, low], axis=0)[:, skip:]
                right = jnp.concatenate([high, mid, high, low, mid, high], axis=0)[:, skip:]
                product = lax.dot_general(left, right, (((0,), (0,)), ((), ())), preferred_element_type=jnp.float32)
                if start < half:
                    work[m, start:half, :] = work[m, start:half, :] - product[start:half, :]
                    work[m, half:, half:] = work[m, half:, half:] - product[half:, half:]
                else:
                    work[m, start:, half:] = work[m, start:, half:] - product[start - half :, :]
    wide = first.shape[0]
    begin = pl.multiple_of(place[0] * wide, wide)
    i = lax.broadcasted_iota(jnp.int32, (wide, n), 0) + begin
    j = lax.broadcasted_iota(jnp.int32, (wide, n), 1)
    for m, out in enumerate((first, second, third)):
        out[...] = jnp.where(j >= i, upper[m, pl.ds(begin, wide), :], 0.0)


def cholesky(place, slabs, wide):
    half = slabs.shape[3]
    whole = pl.BlockSpec(memory_space=pltpu.VMEM)
    return pl.pallas_call(
        cholesky_kernel,
        out_shape=(jax.ShapeDtypeStruct((wide, 2 * half), jnp.float32),) * 3,
        in_specs=[pl.BlockSpec(memory_space=pltpu.SMEM), whole],
        out_specs=(whole,) * 3,
        scratch_shapes=[pltpu.VMEM((3, 2 * half, 2 * half), jnp.float32)] * 2,
        compiler_params=pltpu.CompilerParams(vmem_limit_bytes=32 * MIB),
        name="cholesky",
    )(place, slabs)


def edge(positions, sketch):
    high = lax.reduce_precision(positions, 8, 7)
    rest = positions - high
    mid = lax.reduce_precision(rest, 8, 7)
    parts = jnp.stack([high, mid, rest - mid], axis=1).reshape(9, -1).astype(jnp.bfloat16)
    return jnp.concatenate([sketch, jnp.pad(parts, ((0, 7), (0, 0)))], axis=0)


def on_device(positions, sketch, near):
    slices, rows = sketch.shape
    margin = H * CS
    clus = ("tree", "child")
    count = lax.axis_size(clus)
    shares = lax.axis_size("sk")
    forward = [(i, i + 1) for i in range(count - 1)]
    backward = [(i + 1, i) for i in range(count - 1)]
    low = lax.ppermute(edge(positions[:, -margin:], sketch[:, -margin:]), clus, forward)
    high = lax.ppermute(edge(positions[:, :margin], sketch[:, :margin]), clus, backward)
    image, rounded = near_field(positions, sketch, low, high, near.T, shares)
    traded = lax.all_to_all(rounded, "sk", split_axis=0, concat_axis=0, tiled=True)
    gram = partial_gram(traded, 1.0 / rows)
    family = FAMILY * shares
    slab = gram.reshape(family, -1, gram.shape[1])
    parts = lax.all_to_all(slab, ("child", "sk"), split_axis=0, concat_axis=0, tiled=True)
    sums = combine(parts, FAMILY, shares)
    sums = sums.reshape(family, 3 * slab.shape[1], slab.shape[2])
    slabs = lax.all_to_all(sums, ("child", "sk"), split_axis=0, concat_axis=0, tiled=True)
    slabs = slabs.reshape(family, 3, slab.shape[1], slab.shape[2])
    place = lax.axis_index("sk").astype(jnp.int32).reshape(1)
    return (image, *(factor.T for factor in cholesky(place, slabs, slices)))


def solution(mesh):
    clusters, shares = mesh.devices.shape
    split = Mesh(mesh.devices.reshape(clusters // FAMILY, FAMILY, shares), ("tree", "child", "sk"))
    clus = ("tree", "child")
    return jax.shard_map(
        on_device,
        mesh=split,
        in_specs=(P(None, clus), P("sk", clus), P(clus, None)),
        out_specs=(P("sk", clus), P(clus, "sk"), P(clus, "sk"), P(clus, "sk")),
        check_vma=False,
    )
```

```python
import functools
import math

import jax
import jax.numpy as jnp
from jax import lax
from jax.experimental import pallas as pl
from jax.experimental.pallas import tpu as pltpu
from jax.sharding import Mesh
from jax.sharding import PartitionSpec as P

CS = 256
H = 4
MIB = 2**20
RATE = math.sqrt(3.0) / 0.3
NUGGET = 1.0
FAMILY = 4
UNROLL = 4
PANEL = 16
SHIFT = 64


def near_field_kernel(
    pos_far, sk, low, high, near_far, image, rounded, pos, near, across, along, cols, acc, held, todo, arrived
):
    slices, rows = sk.shape
    own = rows // CS
    half = CS // 2
    fetch_pos = pltpu.make_async_copy(pos_far, pos, arrived.at[0])
    fetch_near = pltpu.make_async_copy(near_far, near, arrived.at[1])
    fetch_pos.start()
    fetch_near.start()
    last = own + 2 * H

    def joined(block):
        parts = [block[slices + r : slices + r + 1, :].astype(jnp.float32) for r in range(9)]
        return jnp.concatenate([parts[r] + parts[r + 1] + parts[r + 2] for r in (0, 3, 6)], axis=0)

    def copy_along(slot):
        for r in range(3):
            along[slot, :, r * 128 : (r + 1) * 128] = jnp.broadcast_to(across[slot, r : r + 1], (128, CS)).T

    for slot in range(last):
        if slot < H:
            a = slot * CS
            block = low[:slices, a : a + CS]
            across[slot] = joined(low[:, a : a + CS])
        elif slot < H + own:
            block = sk[:, (slot - H) * CS : (slot - H + 1) * CS]
        else:
            a = (slot - H - own) * CS
            block = high[:slices, a : a + CS]
            across[slot] = joined(high[:, a : a + CS])
        cols[slot] = block
        acc[slot] = jnp.zeros((slices, CS), jnp.float32)
    fetch_pos.wait()
    for c in range(own):
        across[c + H] = pos[:, c * CS : (c + 1) * CS]
    cols[last] = jnp.zeros((slices, CS), jnp.bfloat16)
    along[last] = jnp.zeros((CS, 384), jnp.float32)
    across[last] = jnp.zeros((3, CS), jnp.float32)
    for slot in range(H, H + 3):
        copy_along(slot)
    for slot in range(H + own, last):
        copy_along(slot)

    def tile(c, s, i=0, j=0, size=CS):
        squared = 1e-30
        for r in range(3):
            point = along[s, i : i + size, r * 128 : (r + 1) * 128]
            if size > 128:
                point = jnp.concatenate([point, point], axis=1)
            diff = point - across[c, r : r + 1, j : j + size]
            squared = squared + diff * diff
        dist = squared * lax.rsqrt(squared)
        return ((1.0 + RATE * dist) * jnp.exp2(dist * (-RATE * math.log2(math.e)))).astype(jnp.bfloat16)

    def product(x, t):
        return jnp.dot(x, t, preferred_element_type=jnp.float32)

    def product_t(x, t):
        return lax.dot_general(x, t, (((1,), (1,)), ((), ())), preferred_element_type=jnp.float32)

    fetch_near.wait()
    count = jnp.int32(UNROLL)
    for s in range(H):
        for d in range(s + 1, H + 1):
            todo[count] = (s - d + H) * SHIFT + s + H
            count = count + near[H - d, s]

    def close_products(c, buf):
        x = cols[c]
        t = held[buf + 1]
        ahead = product(cols[c + 1], t)
        acc[c] = acc[c] + (product(x, held[buf]) + ahead)
        acc[c + 1] = acc[c + 1] + product_t(x, t)

    def close_tiles(c, buf):
        held[buf, :half, :half] = tile(c, c, 0, 0, half)
        corner = tile(c, c, 0, half, half)
        held[buf, :half, half:] = corner
        held[buf, half:, :half] = corner.T
        held[buf, half:, half:] = tile(c, c, half, half, half)
        held[buf + 1] = tile(c, c + 1)

    def close_step(i, count):
        c = i * 2 + H
        for u in range(2):
            close_products(c - 2 + u, 2 * u)
        for u in range(2):
            for d in range(2, H + 1):
                todo[count] = (c + u) * SHIFT + c + u + d
                count = count + near[H + d, c + u - H]
            copy_along(c + u + 3)
            close_tiles(c + u, 2 * u)
        return count

    held[...] = jnp.zeros(held.shape, jnp.bfloat16)
    count = lax.fori_loop(0, own // 2, close_step, count)
    for u in range(2):
        close_products(H + own - 2 + u, 2 * u)
    for slot in range(H):
        copy_along(slot)
    for i in range(UNROLL):
        todo[i] = last * (SHIFT + 1)
        todo[count + i] = last * (SHIFT + 1)

    def far_products(i):
        for u in range(UNROLL):
            code = todo[i * UNROLL + u]
            c, s = code // SHIFT, code % SHIFT
            t = held[u]
            acc[c] = acc[c] + product(cols[s], t)
            acc[s] = acc[s] + product_t(cols[c], t)

    def far_step(i, carry):
        far_products(i - 1)
        for u in range(UNROLL):
            code = todo[i * UNROLL + u]
            held[u] = tile(code // SHIFT, code % SHIFT)
        return carry

    steps = (count + UNROLL - 1) // UNROLL
    lax.fori_loop(1, steps, far_step, 0)
    far_products(steps - 1)

    per = own // rounded.shape[0]
    for c in range(own):
        value = acc[c + H] * (8.0 / CS) + NUGGET * cols[c + H].astype(jnp.float32)
        image[:, c * CS : (c + 1) * CS] = value
        rounded[c // per, :, (c % per) * CS : (c % per + 1) * CS] = value.astype(jnp.bfloat16)


def near_field(pos, sk, low, high, near, shares):
    slices, rows = sk.shape
    slots = rows // CS + 2 * H + 1
    whole = pl.BlockSpec(memory_space=pltpu.VMEM)
    far = pl.BlockSpec(memory_space=pltpu.HBM)
    return pl.pallas_call(
        near_field_kernel,
        out_shape=(
            jax.ShapeDtypeStruct((slices, rows), jnp.float32),
            jax.ShapeDtypeStruct((shares, slices, rows // shares), jnp.bfloat16),
        ),
        in_specs=[far, whole, whole, whole, far],
        out_specs=(whole, whole),
        scratch_shapes=[
            pltpu.VMEM(pos.shape, jnp.float32),
            pltpu.SMEM(near.shape, jnp.int32),
            pltpu.VMEM((slots, 3, CS), jnp.float32),
            pltpu.VMEM((slots, CS, 3 * 128), jnp.float32),
            pltpu.VMEM((slots, slices, CS), jnp.bfloat16),
            pltpu.VMEM((slots, slices, CS), jnp.float32),
            pltpu.VMEM((UNROLL, CS, CS), jnp.bfloat16),
            pltpu.SMEM((slots * H + 4 * UNROLL,), jnp.int32),
            pltpu.SemaphoreType.DMA((2,)),
        ],
        compiler_params=pltpu.CompilerParams(vmem_limit_bytes=36 * MIB),
        name="near_field",
    )(pos, sk, low, high, near)


def gram_kernel(points, out, *, scale):
    whole = points[...].reshape(-1, points.shape[-1])
    half = whole.shape[0] // 2
    part = half // 2
    product = lax.dot_general(whole, whole, (((1,), (1,)), ((), ())), preferred_element_type=jnp.float32) * scale
    lane = lax.broadcasted_iota(jnp.int32, (part, half), 1)
    corner = pltpu.roll(product[half + part :, half:], part, 1)
    mixed = jnp.where(lane < part, corner, product[part:half, :half])
    for i in range(out.shape[0]):
        out[i, :part] = product[:part, :half]
        out[i, part : 2 * part] = product[:part, half:]
        out[i, 2 * part : 3 * part] = product[part:half, half:]
        out[i, 3 * part : 4 * part] = product[half : half + part, half:]
        out[i, 4 * part :] = mixed


def partial_gram(points, scale, copies):
    half = points.shape[0] * points.shape[1] // 2
    return pl.pallas_call(
        lambda points, out: gram_kernel(points, out, scale=scale),
        out_shape=jax.ShapeDtypeStruct((copies, 5 * half // 2, half), jnp.float32),
        compiler_params=pltpu.CompilerParams(vmem_limit_bytes=32 * MIB),
        name="partial_gram",
    )(points)


def pieces(value):
    high = value.astype(jnp.bfloat16)
    rest = value - high.astype(jnp.float32)
    mid = rest.astype(jnp.bfloat16)
    low = (rest - mid.astype(jnp.float32)).astype(jnp.bfloat16)
    return high, mid, low


def cholesky_kernel(place, *refs, mats, averages):
    grams, outs, (work, upper) = refs[: -mats - 2], refs[-mats - 2 : -2], refs[-2:]
    half = work.shape[1] // 2
    part = half // 2
    n = 2 * half
    for m in range(mats):
        for block in range(5):
            rows = slice(block * part, (block + 1) * part)
            value = grams[0][rows]
            if averages:
                value = (value + grams[1][rows]) * 0.5
                if m == 1:
                    value = (value + (grams[2][rows] + grams[3][rows]) * 0.5) * 0.5
            if block == 0:
                work[m, :part, :half] = value
            elif block == 1:
                work[m, :part, half:] = value
            elif block == 2:
                work[m, part:half, half:] = value
            elif block == 3:
                work[m, half : half + part, half:] = value
            else:
                work[m, part:half, :half] = value
                work[m, half + part :, half:] = pltpu.roll(value, part, 1)
    for m in range(mats):
        upper[m, half:, :half] = jnp.zeros((half, half), jnp.float32)
    rowid = lax.broadcasted_iota(jnp.int32, (8, 128), 0)
    spread = lambda row: jnp.broadcast_to(row, (8, 128))
    for j0 in range(0, n, PANEL):
        lane0 = 0 if j0 < half else half
        width = (n - lane0) // 128
        rows, cols, scale = [], [], []
        for m in range(mats):
            block = work[m, j0 : j0 + PANEL, lane0:]
            rows.append(
                [[block[8 * h : 8 * h + 8, 128 * w : 128 * w + 128] for w in range(width)] for h in range(2)]
            )
            at = j0 - lane0
            cols.append(
                [[spread(block[8 * h : 8 * h + 8, at + c : at + c + 1]) for h in range(2)] for c in range(PANEL)]
            )
            scale.append([jnp.zeros((8, 128), jnp.float32) for h in range(2)])
        for q in range(PANEL):
            hq, r = q // 8, q % 8
            for m in range(mats):
                inv = lax.rsqrt(spread(cols[m][q][hq][r : r + 1, :]))
                scale[m][hq] = jnp.where(rowid == r, inv, scale[m][hq])
                inv2 = inv * inv
                factor = [None, None]
                for h in range(hq, 2):
                    f = cols[m][q][h] * inv2
                    factor[h] = jnp.where(rowid > r, f, 0.0) if h == hq else f
                for c in range(q + 1, PANEL):
                    row = spread(cols[m][c][hq][r : r + 1, :])
                    for h in range(hq, 2):
                        cols[m][c][h] = cols[m][c][h] - factor[h] * row
                for w in range(width):
                    row = spread(rows[m][hq][w][r : r + 1, :])
                    for h in range(hq, 2):
                        rows[m][h][w] = rows[m][h][w] - factor[h] * row
        start = j0 + PANEL
        for m in range(mats):
            done = jnp.concatenate(
                [
                    jnp.concatenate([rows[m][h][w] * scale[m][h] for w in range(width)], axis=1)
                    for h in range(2)
                ],
                axis=0,
            )
            upper[m, j0 : j0 + PANEL, lane0:] = done
            if start < n:
                high, mid, low = pieces(done)
                left = jnp.concatenate([high, high, mid, high, mid, low], axis=0)
                right = jnp.concatenate([high, mid, high, low, mid, high], axis=0)
                skip = (0 if start < half else half) - lane0
                product = lax.dot_general(
                    left[:, skip:], right[:, skip:], (((0,), (0,)), ((), ())), preferred_element_type=jnp.float32
                )
                if start < half:
                    work[m, start:half, :] = work[m, start:half, :] - product[start:half, :]
                    work[m, half:, half:] = work[m, half:, half:] - product[half:, half:]
                else:
                    work[m, start:, half:] = work[m, start:, half:] - product[start - half :, :]
    wide = outs[0].shape[0]
    begin = pl.multiple_of(place[0] * wide, wide)
    i = lax.broadcasted_iota(jnp.int32, (wide, n), 0) + begin
    j = lax.broadcasted_iota(jnp.int32, (wide, n), 1)
    for m, out in enumerate(outs):
        out[...] = jnp.where(j >= i, upper[m, pl.ds(begin, wide), :], 0.0)


def cholesky(place, grams, wide, mats, name):
    half = grams[0].shape[1]
    whole = pl.BlockSpec(memory_space=pltpu.VMEM)
    kernel = functools.partial(cholesky_kernel, mats=mats, averages=len(grams) > 1)
    return pl.pallas_call(
        kernel,
        out_shape=(jax.ShapeDtypeStruct((wide, 2 * half), jnp.float32),) * mats,
        in_specs=[pl.BlockSpec(memory_space=pltpu.SMEM)] + [whole] * len(grams),
        out_specs=(whole,) * mats,
        scratch_shapes=[pltpu.VMEM((mats, 2 * half, 2 * half), jnp.float32)] * 2,
        compiler_params=pltpu.CompilerParams(vmem_limit_bytes=32 * MIB),
        name=name,
    )(place, *grams)


def edge(positions, sketch):
    high = lax.reduce_precision(positions, 8, 7)
    rest = positions - high
    mid = lax.reduce_precision(rest, 8, 7)
    parts = jnp.stack([high, mid, rest - mid], axis=1).reshape(9, -1).astype(jnp.bfloat16)
    return jnp.concatenate([sketch, jnp.pad(parts, ((0, 7), (0, 0)))], axis=0)


def on_device(positions, sketch, near):
    slices, rows = sketch.shape
    margin = H * CS
    clus = ("tree", "child")
    count = lax.axis_size(clus)
    shares = lax.axis_size("sk")
    forward = [(i, i + 1) for i in range(count - 1)]
    backward = [(i + 1, i) for i in range(count - 1)]
    low = lax.ppermute(edge(positions[:, -margin:], sketch[:, -margin:]), clus, forward)
    high = lax.ppermute(edge(positions[:, :margin], sketch[:, :margin]), clus, backward)
    image, rounded = near_field(positions, sketch, low, high, near.T, shares)
    traded = lax.all_to_all(rounded, "sk", split_axis=0, concat_axis=0, tiled=True)
    shared = partial_gram(traded, 1.0 / rows, shares)
    parts = lax.all_to_all(shared, "sk", split_axis=0, concat_axis=0, tiled=True)
    node = jnp.sum(parts, axis=0)
    siblings = [lax.ppermute(node, "child", [(i, i ^ d) for i in range(FAMILY)]) for d in range(1, FAMILY)]
    place = lax.axis_index("sk").astype(jnp.int32).reshape(1)
    first = cholesky(place, [node], slices, 1, "node_factor")
    others = cholesky(place, [node, *siblings], slices, 2, "upper_factors")
    return (image, *(factor.T for factor in (*first, *others)))


def solution(mesh):
    clusters, shares = mesh.devices.shape
    split = Mesh(mesh.devices.reshape(clusters // FAMILY, FAMILY, shares), ("tree", "child", "sk"))
    clus = ("tree", "child")
    return jax.shard_map(
        on_device,
        mesh=split,
        in_specs=(P(None, clus), P("sk", clus), P(clus, None)),
        out_specs=(P("sk", clus), P(clus, "sk"), P(clus, "sk"), P(clus, "sk")),
        check_vma=False,
    )
```

```python
import math

import jax
import jax.numpy as jnp
from jax import lax
from jax.experimental import pallas as pl
from jax.experimental.pallas import tpu as pltpu
from jax.sharding import Mesh
from jax.sharding import PartitionSpec as P

CS = 256
H = 4
MIB = 2**20
RATE = math.sqrt(3.0) / 0.3
NUGGET = 1.0
FAMILY = 4
UNROLL = 4
PANEL = 16
SHIFT = 64


def near_field_kernel(
    pos, sk, low, high, near_far, image, rounded, near, across, along, cols, acc, held, todo, arrived
):
    slices, rows = sk.shape
    own = rows // CS
    half = CS // 2
    fetch_near = pltpu.make_async_copy(near_far, near, arrived)
    fetch_near.start()
    last = own + 2 * H

    def joined(block):
        parts = [block[slices + r : slices + r + 1, :].astype(jnp.float32) for r in range(9)]
        return jnp.concatenate([parts[r] + parts[r + 1] + parts[r + 2] for r in (0, 3, 6)], axis=0)

    def copy_along(slot):
        for r in range(3):
            along[slot, :, r * 128 : (r + 1) * 128] = jnp.broadcast_to(across[slot, r : r + 1], (128, CS)).T

    for slot in range(last):
        if slot < H:
            a = slot * CS
            block = low[:slices, a : a + CS]
            across[slot] = joined(low[:, a : a + CS])
        elif slot < H + own:
            block = sk[:, (slot - H) * CS : (slot - H + 1) * CS]
        else:
            a = (slot - H - own) * CS
            block = high[:slices, a : a + CS]
            across[slot] = joined(high[:, a : a + CS])
        cols[slot] = block
        acc[slot] = jnp.zeros((slices, CS), jnp.float32)
    for c in range(own):
        across[c + H] = pos[c]
    cols[last] = jnp.zeros((slices, CS), jnp.bfloat16)
    along[last] = jnp.zeros((CS, 384), jnp.float32)
    across[last] = jnp.zeros((3, CS), jnp.float32)
    for slot in range(H, H + 3):
        copy_along(slot)
    for slot in range(H + own, last):
        copy_along(slot)

    def tile(c, s, i=0, j=0, size=CS):
        squared = 1e-30
        for r in range(3):
            point = along[s, i : i + size, r * 128 : (r + 1) * 128]
            if size > 128:
                point = jnp.concatenate([point, point], axis=1)
            diff = point - across[c, r : r + 1, j : j + size]
            squared = squared + diff * diff
        dist = squared * lax.rsqrt(squared)
        return ((1.0 + RATE * dist) * jnp.exp2(dist * (-RATE * math.log2(math.e)))).astype(jnp.bfloat16)

    def product(x, t):
        return jnp.dot(x, t, preferred_element_type=jnp.float32)

    def product_t(x, t):
        return lax.dot_general(x, t, (((1,), (1,)), ((), ())), preferred_element_type=jnp.float32)

    fetch_near.wait()
    count = jnp.int32(UNROLL)
    for s in range(H):
        for d in range(s + 1, H + 1):
            todo[count] = (s - d + H) * SHIFT + s + H
            count = count + near[s, H - d]

    def close_products(c, buf):
        x = cols[c]
        t = held[buf + 1]
        ahead = product(cols[c + 1], t)
        acc[c] = acc[c] + (product(x, held[buf]) + ahead)
        acc[c + 1] = acc[c + 1] + product_t(x, t)

    def close_tiles(c, buf):
        held[buf, :half, :half] = tile(c, c, 0, 0, half)
        corner = tile(c, c, 0, half, half)
        held[buf, :half, half:] = corner
        held[buf, half:, :half] = corner.T
        held[buf, half:, half:] = tile(c, c, half, half, half)
        held[buf + 1] = tile(c, c + 1)

    def close_step(i, count):
        c = i * 2 + H
        for u in range(2):
            close_products(c - 2 + u, 2 * u)
        for u in range(2):
            for d in range(2, H + 1):
                todo[count] = (c + u) * SHIFT + c + u + d
                count = count + near[c + u - H, H + d]
            copy_along(c + u + 3)
            close_tiles(c + u, 2 * u)
        return count

    held[...] = jnp.zeros(held.shape, jnp.bfloat16)
    count = lax.fori_loop(0, own // 2, close_step, count)
    for u in range(2):
        close_products(H + own - 2 + u, 2 * u)
    for slot in range(H):
        copy_along(slot)
    for i in range(UNROLL):
        todo[i] = last * (SHIFT + 1)
        todo[count + i] = last * (SHIFT + 1)

    def far_products(i):
        for u in range(UNROLL):
            code = todo[i * UNROLL + u]
            c, s = code // SHIFT, code % SHIFT
            t = held[u]
            acc[c] = acc[c] + product(cols[s], t)
            acc[s] = acc[s] + product_t(cols[c], t)

    def far_step(i, carry):
        far_products(i - 1)
        for u in range(UNROLL):
            code = todo[i * UNROLL + u]
            held[u] = tile(code // SHIFT, code % SHIFT)
        return carry

    steps = (count + UNROLL - 1) // UNROLL
    lax.fori_loop(1, steps, far_step, 0)
    far_products(steps - 1)

    per = own // rounded.shape[0]
    for c in range(own):
        value = acc[c + H] * (8.0 / CS) + NUGGET * cols[c + H].astype(jnp.float32)
        image[:, c * CS : (c + 1) * CS] = value
        rounded[c // per, :, (c % per) * CS : (c % per + 1) * CS] = value.astype(jnp.bfloat16)


def near_field(pos, sk, low, high, near, shares):
    slices, rows = sk.shape
    slots = rows // CS + 2 * H + 1
    whole = pl.BlockSpec(memory_space=pltpu.VMEM)
    far = pl.BlockSpec(memory_space=pltpu.HBM)
    return pl.pallas_call(
        near_field_kernel,
        out_shape=(
            jax.ShapeDtypeStruct((slices, rows), jnp.float32),
            jax.ShapeDtypeStruct((shares, slices, rows // shares), jnp.bfloat16),
        ),
        in_specs=[whole, whole, whole, whole, far],
        out_specs=(whole, whole),
        scratch_shapes=[
            pltpu.SMEM(near.shape, jnp.int32),
            pltpu.VMEM((slots, 3, CS), jnp.float32),
            pltpu.VMEM((slots, CS, 3 * 128), jnp.float32),
            pltpu.VMEM((slots, slices, CS), jnp.bfloat16),
            pltpu.VMEM((slots, slices, CS), jnp.float32),
            pltpu.VMEM((UNROLL, CS, CS), jnp.bfloat16),
            pltpu.SMEM((slots * H + 4 * UNROLL,), jnp.int32),
            pltpu.SemaphoreType.DMA,
        ],
        compiler_params=pltpu.CompilerParams(vmem_limit_bytes=36 * MIB),
        name="near_field",
    )(pos, sk, low, high, near)


def gram_kernel(points, out, *, scale):
    whole = points[...].reshape(-1, points.shape[-1])
    half = whole.shape[0] // 2
    part = half // 2
    product = lax.dot_general(whole, whole, (((1,), (1,)), ((), ())), preferred_element_type=jnp.float32) * scale
    lane = lax.broadcasted_iota(jnp.int32, (part, half), 1)
    corner = pltpu.roll(product[half + part :, half:], part, 1)
    mixed = jnp.where(lane < part, corner, product[part:half, :half])
    for i in range(out.shape[0]):
        out[i, :part] = product[:part, :half]
        out[i, part : 2 * part] = product[:part, half:]
        out[i, 2 * part : 3 * part] = product[part:half, half:]
        out[i, 3 * part : 4 * part] = product[half : half + part, half:]
        out[i, 4 * part :] = mixed


def partial_gram(points, scale, copies):
    half = points.shape[0] * points.shape[1] // 2
    return pl.pallas_call(
        lambda points, out: gram_kernel(points, out, scale=scale),
        out_shape=jax.ShapeDtypeStruct((copies, 5 * half // 2, half), jnp.float32),
        compiler_params=pltpu.CompilerParams(vmem_limit_bytes=32 * MIB),
        name="partial_gram",
    )(points)


def pieces(value):
    high = value.astype(jnp.bfloat16)
    rest = value - high.astype(jnp.float32)
    mid = rest.astype(jnp.bfloat16)
    low = (rest - mid.astype(jnp.float32)).astype(jnp.bfloat16)
    return high, mid, low


def cholesky_kernel(place, grams, *refs):
    outs, (work, upper) = refs[:-2], refs[-2:]
    mats = len(outs)
    half = work.shape[1] // 2
    part = half // 2
    n = 2 * half
    for m in range(mats):
        for block in range(5):
            value = grams[m, block * part : (block + 1) * part]
            if block == 0:
                work[m, :part, :half] = value
            elif block == 1:
                work[m, :part, half:] = value
            elif block == 2:
                work[m, part:half, half:] = value
            elif block == 3:
                work[m, half : half + part, half:] = value
            else:
                work[m, part:half, :half] = value
                work[m, half + part :, half:] = pltpu.roll(value, part, 1)
    for m in range(mats):
        upper[m, half:, :half] = jnp.zeros((half, half), jnp.float32)
    rowid = lax.broadcasted_iota(jnp.int32, (8, 128), 0)
    spread = lambda row: jnp.broadcast_to(row, (8, 128))
    for j0 in range(0, n, PANEL):
        lane0 = 0 if j0 < half else half
        width = (n - lane0) // 128
        rows, cols, scale = [], [], []
        for m in range(mats):
            block = work[m, j0 : j0 + PANEL, lane0:]
            rows.append(
                [[block[8 * h : 8 * h + 8, 128 * w : 128 * w + 128] for w in range(width)] for h in range(2)]
            )
            at = j0 - lane0
            cols.append(
                [[spread(block[8 * h : 8 * h + 8, at + c : at + c + 1]) for h in range(2)] for c in range(PANEL)]
            )
            scale.append([jnp.zeros((8, 128), jnp.float32) for h in range(2)])
        for q in range(PANEL):
            hq, r = q // 8, q % 8
            for m in range(mats):
                inv = lax.rsqrt(spread(cols[m][q][hq][r : r + 1, :]))
                scale[m][hq] = jnp.where(rowid == r, inv, scale[m][hq])
                inv2 = inv * inv
                factor = [None, None]
                for h in range(hq, 2):
                    f = cols[m][q][h] * inv2
                    factor[h] = jnp.where(rowid > r, f, 0.0) if h == hq else f
                for c in range(q + 1, PANEL):
                    row = spread(cols[m][c][hq][r : r + 1, :])
                    for h in range(hq, 2):
                        cols[m][c][h] = cols[m][c][h] - factor[h] * row
                for w in range(width):
                    row = spread(rows[m][hq][w][r : r + 1, :])
                    for h in range(hq, 2):
                        rows[m][h][w] = rows[m][h][w] - factor[h] * row
        start = j0 + PANEL
        for m in range(mats):
            done = jnp.concatenate(
                [
                    jnp.concatenate([rows[m][h][w] * scale[m][h] for w in range(width)], axis=1)
                    for h in range(2)
                ],
                axis=0,
            )
            upper[m, j0 : j0 + PANEL, lane0:] = done
            if start < n:
                high, mid, low = pieces(done)
                left = jnp.concatenate([high, high, mid, high, mid, low], axis=0)
                right = jnp.concatenate([high, mid, high, low, mid, high], axis=0)
                skip = (0 if start < half else half) - lane0
                product = lax.dot_general(
                    left[:, skip:], right[:, skip:], (((0,), (0,)), ((), ())), preferred_element_type=jnp.float32
                )
                if start < half:
                    work[m, start:half, :] = work[m, start:half, :] - product[start:half, :]
                    work[m, half:, half:] = work[m, half:, half:] - product[half:, half:]
                else:
                    work[m, start:, half:] = work[m, start:, half:] - product[start - half :, :]
    wide = outs[0].shape[0]
    begin = pl.multiple_of(place[0] * wide, wide)
    i = lax.broadcasted_iota(jnp.int32, (wide, n), 0) + begin
    j = lax.broadcasted_iota(jnp.int32, (wide, n), 1)
    for m, out in enumerate(outs):
        out[...] = jnp.where(j >= i, upper[m, pl.ds(begin, wide), :], 0.0)


def cholesky(place, grams, wide):
    mats, half = grams.shape[0], grams.shape[2]
    whole = pl.BlockSpec(memory_space=pltpu.VMEM)
    return pl.pallas_call(
        cholesky_kernel,
        out_shape=(jax.ShapeDtypeStruct((wide, 2 * half), jnp.float32),) * mats,
        in_specs=[pl.BlockSpec(memory_space=pltpu.SMEM), whole],
        out_specs=(whole,) * mats,
        scratch_shapes=[pltpu.VMEM((mats, 2 * half, 2 * half), jnp.float32)] * 2,
        compiler_params=pltpu.CompilerParams(vmem_limit_bytes=32 * MIB),
        name="cholesky",
    )(place, grams)


def edge(positions, sketch):
    high = lax.reduce_precision(positions, 8, 7)
    rest = positions - high
    mid = lax.reduce_precision(rest, 8, 7)
    parts = jnp.stack([high, mid, rest - mid], axis=1).reshape(9, -1).astype(jnp.bfloat16)
    return jnp.concatenate([sketch, jnp.pad(parts, ((0, 7), (0, 0)))], axis=0)


def on_device(positions, sketch, near):
    slices, rows = sketch.shape
    margin = H * CS
    clus = ("tree", "child")
    count = lax.axis_size(clus)
    shares = lax.axis_size("sk")
    forward = [(i, i + 1) for i in range(count - 1)]
    backward = [(i + 1, i) for i in range(count - 1)]
    low = lax.ppermute(edge(positions[:, -margin:], sketch[:, -margin:]), clus, forward)
    high = lax.ppermute(edge(positions[:, :margin], sketch[:, :margin]), clus, backward)
    by_cluster = positions.reshape(3, -1, CS).transpose(1, 0, 2)
    image, rounded = near_field(by_cluster, sketch, low, high, near, shares)
    traded = lax.all_to_all(rounded, "sk", split_axis=0, concat_axis=0, tiled=True)
    shared = partial_gram(traded, 1.0 / rows, shares)
    parts = lax.all_to_all(shared, "sk", split_axis=0, concat_axis=0, tiled=True)
    node = jnp.sum(parts, axis=0)
    sibling = lambda value, d: lax.ppermute(value, "child", [(i, i ^ d) for i in range(FAMILY)])
    pair = (node + sibling(node, 1)) * 0.5
    group = (pair + sibling(pair, 2)) * 0.5
    place = lax.axis_index("sk").astype(jnp.int32).reshape(1)
    factors = cholesky(place, jnp.stack([node, pair, group]), slices)
    return (image, *(factor.T for factor in factors))


def solution(mesh):
    clusters, shares = mesh.devices.shape
    split = Mesh(mesh.devices.reshape(clusters // FAMILY, FAMILY, shares), ("tree", "child", "sk"))
    clus = ("tree", "child")
    return jax.shard_map(
        on_device,
        mesh=split,
        in_specs=(P(None, clus), P("sk", clus), P(clus, None)),
        out_specs=(P("sk", clus), P(clus, "sk"), P(clus, "sk"), P(clus, "sk")),
        check_vma=False,
    )
```

```python
import math

import jax
import jax.numpy as jnp
from jax import lax
from jax.experimental import pallas as pl
from jax.experimental.pallas import tpu as pltpu
from jax.sharding import Mesh
from jax.sharding import PartitionSpec as P

CS = 256
H = 4
MIB = 2**20
RATE = math.sqrt(3.0) / 0.3
NUGGET = 1.0
FAMILY = 4
UNROLL = 4
PANEL = 16
SHIFT = 64


def near_field_kernel(
    pos, sk, low, high, near_far, image, rounded, near, across, along, cols, acc, held, todo, arrived
):
    slices, rows = sk.shape
    own = rows // CS
    half = CS // 2
    fetch_near = pltpu.make_async_copy(near_far, near, arrived)
    fetch_near.start()
    last = own + 2 * H

    def joined(block):
        parts = [block[slices + r : slices + r + 1, :].astype(jnp.float32) for r in range(9)]
        return jnp.concatenate([parts[r] + parts[r + 1] + parts[r + 2] for r in (0, 3, 6)], axis=0)

    def copy_along(slot):
        for r in range(3):
            along[slot, :, r * 128 : (r + 1) * 128] = jnp.broadcast_to(across[slot, r : r + 1], (128, CS)).T

    for slot in range(last):
        if slot < H:
            a = slot * CS
            block = low[:slices, a : a + CS]
            across[slot] = joined(low[:, a : a + CS])
        elif slot < H + own:
            block = sk[:, (slot - H) * CS : (slot - H + 1) * CS]
        else:
            a = (slot - H - own) * CS
            block = high[:slices, a : a + CS]
            across[slot] = joined(high[:, a : a + CS])
        cols[slot] = block
        acc[slot] = jnp.zeros((slices, CS), jnp.float32)
    for c in range(own):
        across[c + H] = pos[c, :3]
    cols[last] = jnp.zeros((slices, CS), jnp.bfloat16)
    along[last] = jnp.zeros((CS, 384), jnp.float32)
    across[last] = jnp.zeros((3, CS), jnp.float32)
    for slot in range(H, H + 3):
        copy_along(slot)
    for slot in range(H + own, last):
        copy_along(slot)

    def tile(c, s, i=0, j=0, size=CS):
        squared = 1e-30
        for r in range(3):
            point = along[s, i : i + size, r * 128 : (r + 1) * 128]
            if size > 128:
                point = jnp.concatenate([point, point], axis=1)
            diff = point - across[c, r : r + 1, j : j + size]
            squared = squared + diff * diff
        dist = squared * lax.rsqrt(squared)
        return ((1.0 + RATE * dist) * jnp.exp2(dist * (-RATE * math.log2(math.e)))).astype(jnp.bfloat16)

    def product(x, t):
        return jnp.dot(x, t, preferred_element_type=jnp.float32)

    def product_t(x, t):
        return lax.dot_general(x, t, (((1,), (1,)), ((), ())), preferred_element_type=jnp.float32)

    fetch_near.wait()
    count = jnp.int32(UNROLL)
    for s in range(H):
        for d in range(s + 1, H + 1):
            todo[count] = (s - d + H) * SHIFT + s + H
            count = count + near[s, H - d]

    def close_products(c, buf):
        x = cols[c]
        t = held[buf + 1]
        ahead = product(cols[c + 1], t)
        acc[c] = acc[c] + (product(x, held[buf]) + ahead)
        acc[c + 1] = acc[c + 1] + product_t(x, t)

    def close_tiles(c, buf):
        held[buf, :half, :half] = tile(c, c, 0, 0, half)
        corner = tile(c, c, 0, half, half)
        held[buf, :half, half:] = corner
        held[buf, half:, :half] = corner.T
        held[buf, half:, half:] = tile(c, c, half, half, half)
        held[buf + 1] = tile(c, c + 1)

    def close_step(i, count):
        c = i * 2 + H
        for u in range(2):
            close_products(c - 2 + u, 2 * u)
        for u in range(2):
            for d in range(2, H + 1):
                todo[count] = (c + u) * SHIFT + c + u + d
                count = count + near[c + u - H, H + d]
            copy_along(c + u + 3)
            close_tiles(c + u, 2 * u)
        return count

    held[...] = jnp.zeros(held.shape, jnp.bfloat16)
    count = lax.fori_loop(0, own // 2, close_step, count)
    for u in range(2):
        close_products(H + own - 2 + u, 2 * u)
    for slot in range(H):
        copy_along(slot)
    for i in range(UNROLL):
        todo[i] = last * (SHIFT + 1)
        todo[count + i] = last * (SHIFT + 1)

    def far_products(i):
        for u in range(UNROLL):
            code = todo[i * UNROLL + u]
            c, s = code // SHIFT, code % SHIFT
            t = held[u]
            acc[c] = acc[c] + product(cols[s], t)
            acc[s] = acc[s] + product_t(cols[c], t)

    def far_step(i, carry):
        far_products(i - 1)
        for u in range(UNROLL):
            code = todo[i * UNROLL + u]
            held[u] = tile(code // SHIFT, code % SHIFT)
        return carry

    steps = (count + UNROLL - 1) // UNROLL
    lax.fori_loop(1, steps, far_step, 0)
    far_products(steps - 1)

    per = own // rounded.shape[0]
    for c in range(own):
        value = acc[c + H] * (8.0 / CS) + NUGGET * cols[c + H].astype(jnp.float32)
        image[:, c * CS : (c + 1) * CS] = value
        rounded[c // per, :, (c % per) * CS : (c % per + 1) * CS] = value.astype(jnp.bfloat16)


def near_field(pos, sk, low, high, near, shares):
    slices, rows = sk.shape
    slots = rows // CS + 2 * H + 1
    whole = pl.BlockSpec(memory_space=pltpu.VMEM)
    far = pl.BlockSpec(memory_space=pltpu.HBM)
    return pl.pallas_call(
        near_field_kernel,
        out_shape=(
            jax.ShapeDtypeStruct((slices, rows), jnp.float32),
            jax.ShapeDtypeStruct((shares, slices, rows // shares), jnp.bfloat16),
        ),
        in_specs=[whole, whole, whole, whole, far],
        out_specs=(whole, whole),
        scratch_shapes=[
            pltpu.SMEM(near.shape, jnp.int32),
            pltpu.VMEM((slots, 3, CS), jnp.float32),
            pltpu.VMEM((slots, CS, 3 * 128), jnp.float32),
            pltpu.VMEM((slots, slices, CS), jnp.bfloat16),
            pltpu.VMEM((slots, slices, CS), jnp.float32),
            pltpu.VMEM((UNROLL, CS, CS), jnp.bfloat16),
            pltpu.SMEM((slots * H + 4 * UNROLL,), jnp.int32),
            pltpu.SemaphoreType.DMA,
        ],
        compiler_params=pltpu.CompilerParams(vmem_limit_bytes=36 * MIB),
        name="near_field",
    )(pos, sk, low, high, near)


def gram_kernel(points, out, *, scale):
    whole = points[...].reshape(-1, points.shape[-1])
    half = whole.shape[0] // 2
    part = half // 2
    product = lax.dot_general(whole, whole, (((1,), (1,)), ((), ())), preferred_element_type=jnp.float32) * scale
    lane = lax.broadcasted_iota(jnp.int32, (part, half), 1)
    corner = pltpu.roll(product[half + part :, half:], part, 1)
    mixed = jnp.where(lane < part, corner, product[part:half, :half])
    for i in range(out.shape[0]):
        out[i, :part] = product[:part, :half]
        out[i, part : 2 * part] = product[:part, half:]
        out[i, 2 * part : 3 * part] = product[part:half, half:]
        out[i, 3 * part : 4 * part] = product[half : half + part, half:]
        out[i, 4 * part :] = mixed


def partial_gram(points, scale, copies):
    half = points.shape[0] * points.shape[1] // 2
    return pl.pallas_call(
        lambda points, out: gram_kernel(points, out, scale=scale),
        out_shape=jax.ShapeDtypeStruct((copies, 5 * half // 2, half), jnp.float32),
        compiler_params=pltpu.CompilerParams(vmem_limit_bytes=32 * MIB),
        name="partial_gram",
    )(points)


def pieces(value):
    high = value.astype(jnp.bfloat16)
    rest = value - high.astype(jnp.float32)
    mid = rest.astype(jnp.bfloat16)
    low = (rest - mid.astype(jnp.float32)).astype(jnp.bfloat16)
    return high, mid, low


def cholesky_kernel(place, grams, *refs):
    outs, (work, upper) = refs[:-2], refs[-2:]
    mats = len(outs)
    half = work.shape[1] // 2
    part = half // 2
    n = 2 * half
    for m in range(mats):
        for block in range(5):
            value = grams[m, block * part : (block + 1) * part]
            if block == 0:
                work[m, :part, :half] = value
            elif block == 1:
                work[m, :part, half:] = value
            elif block == 2:
                work[m, part:half, half:] = value
            elif block == 3:
                work[m, half : half + part, half:] = value
            else:
                work[m, part:half, :half] = value
                work[m, half + part :, half:] = pltpu.roll(value, part, 1)
    for m in range(mats):
        upper[m, half:, :half] = jnp.zeros((half, half), jnp.float32)
    rowid = lax.broadcasted_iota(jnp.int32, (8, 128), 0)
    spread = lambda row: jnp.broadcast_to(row, (8, 128))
    blank = upper[0, half : half + 8, :half]
    for j0 in range(0, n, PANEL):
        lane0 = 0 if j0 < half else half
        width = (n - lane0) // 128
        rows, cols, scale = [], [], []
        for m in range(mats):
            block = work[m, j0 : j0 + PANEL, lane0:]
            rows.append(
                [[block[8 * h : 8 * h + 8, 128 * w : 128 * w + 128] for w in range(width)] for h in range(2)]
            )
            at = j0 - lane0
            cols.append(
                [[spread(block[8 * h : 8 * h + 8, at + c : at + c + 1]) + blank for h in range(2)] for c in range(PANEL)]
            )
            scale.append([jnp.zeros((8, 128), jnp.float32) for h in range(2)])
        for q in range(PANEL):
            hq, r = q // 8, q % 8
            for m in range(mats):
                inv = lax.rsqrt(spread(cols[m][q][hq][r : r + 1, :]))
                scale[m][hq] = jnp.where(rowid == r, inv, scale[m][hq])
                inv2 = inv * inv
                factor = [None, None]
                for h in range(hq, 2):
                    f = cols[m][q][h] * inv2
                    factor[h] = jnp.where(rowid > r, f, 0.0) if h == hq else f
                for c in range(q + 1, PANEL):
                    row = spread(cols[m][c][hq][r : r + 1, :])
                    for h in range(hq, 2):
                        cols[m][c][h] = cols[m][c][h] - factor[h] * row
                for w in range(width):
                    row = spread(rows[m][hq][w][r : r + 1, :])
                    for h in range(hq, 2):
                        rows[m][h][w] = rows[m][h][w] - factor[h] * row
        start = j0 + PANEL
        for m in range(mats):
            done = jnp.concatenate(
                [
                    jnp.concatenate([rows[m][h][w] * scale[m][h] for w in range(width)], axis=1)
                    for h in range(2)
                ],
                axis=0,
            )
            upper[m, j0 : j0 + PANEL, lane0:] = done
            if start < n:
                high, mid, low = pieces(done)
                left = jnp.concatenate([high, high, mid, high, mid, low], axis=0)
                right = jnp.concatenate([high, mid, high, low, mid, high], axis=0)
                skip = (0 if start < half else half) - lane0
                product = lax.dot_general(
                    left[:, skip:], right[:, skip:], (((0,), (0,)), ((), ())), preferred_element_type=jnp.float32
                )
                if start < half:
                    work[m, start:half, :] = work[m, start:half, :] - product[start:half, :]
                    work[m, half:, half:] = work[m, half:, half:] - product[half:, half:]
                else:
                    work[m, start:, half:] = work[m, start:, half:] - product[start - half :, :]
    wide = outs[0].shape[0]
    begin = pl.multiple_of(place[0] * wide, wide)
    i = lax.broadcasted_iota(jnp.int32, (wide, n), 0) + begin
    j = lax.broadcasted_iota(jnp.int32, (wide, n), 1)
    for m, out in enumerate(outs):
        out[...] = jnp.where(j >= i, upper[m, pl.ds(begin, wide), :], 0.0)


def cholesky(place, grams, wide):
    mats, half = grams.shape[0], grams.shape[2]
    whole = pl.BlockSpec(memory_space=pltpu.VMEM)
    return pl.pallas_call(
        cholesky_kernel,
        out_shape=(jax.ShapeDtypeStruct((wide, 2 * half), jnp.float32),) * mats,
        in_specs=[pl.BlockSpec(memory_space=pltpu.SMEM), whole],
        out_specs=(whole,) * mats,
        scratch_shapes=[pltpu.VMEM((mats, 2 * half, 2 * half), jnp.float32)] * 2,
        compiler_params=pltpu.CompilerParams(vmem_limit_bytes=32 * MIB),
        name="cholesky",
    )(place, grams)


def edge(positions, sketch):
    high = lax.reduce_precision(positions, 8, 7)
    rest = positions - high
    mid = lax.reduce_precision(rest, 8, 7)
    parts = jnp.stack([high, mid, rest - mid], axis=1).reshape(9, -1).astype(jnp.bfloat16)
    return jnp.concatenate([sketch, jnp.pad(parts, ((0, 7), (0, 0)))], axis=0)


def on_device(positions, sketch, near):
    slices, rows = sketch.shape
    margin = H * CS
    clus = ("tree", "child")
    count = lax.axis_size(clus)
    shares = lax.axis_size("sk")
    forward = [(i, i + 1) for i in range(count - 1)]
    backward = [(i + 1, i) for i in range(count - 1)]
    low = lax.ppermute(edge(positions[:, -margin:], sketch[:, -margin:]), clus, forward)
    high = lax.ppermute(edge(positions[:, :margin], sketch[:, :margin]), clus, backward)
    by_cluster = jnp.pad(positions, ((0, 1), (0, 0))).reshape(4, -1, CS).transpose(1, 0, 2)
    image, rounded = near_field(by_cluster, sketch, low, high, near, shares)
    traded = lax.all_to_all(rounded, "sk", split_axis=0, concat_axis=0, tiled=True)
    shared = partial_gram(traded, 1.0 / rows, shares)
    parts = lax.all_to_all(shared, "sk", split_axis=0, concat_axis=0, tiled=True)
    node = jnp.sum(parts, axis=0)
    sibling = lambda value, d: lax.ppermute(value, "child", [(i, i ^ d) for i in range(FAMILY)])
    pair = (node + sibling(node, 1)) * 0.5
    group = (pair + sibling(pair, 2)) * 0.5
    place = lax.axis_index("sk").astype(jnp.int32).reshape(1)
    factors = cholesky(place, jnp.stack([node, pair, group]), slices)
    return (image, *(factor.T for factor in factors))


def solution(mesh):
    clusters, shares = mesh.devices.shape
    split = Mesh(mesh.devices.reshape(clusters // FAMILY, FAMILY, shares), ("tree", "child", "sk"))
    clus = ("tree", "child")
    return jax.shard_map(
        on_device,
        mesh=split,
        in_specs=(P(None, clus), P("sk", clus), P(clus, None)),
        out_specs=(P("sk", clus), P(clus, "sk"), P(clus, "sk"), P(clus, "sk")),
        check_vma=False,
    )
```

```python
import math

import jax
import jax.numpy as jnp
from jax import lax
from jax.experimental import pallas as pl
from jax.experimental.pallas import tpu as pltpu
from jax.sharding import Mesh
from jax.sharding import PartitionSpec as P

CS = 256
H = 4
MIB = 2**20
RATE = math.sqrt(3.0) / 0.3
NUGGET = 1.0
FAMILY = 4
UNROLL = 6
PANEL = 16
SHIFT = 64


def near_field_kernel(
    pos, sk, low, high, near_far, image, rounded, near, across, along, cols, acc, held, todo, arrived
):
    slices, rows = sk.shape
    own = rows // CS
    half = CS // 2
    fetch_near = pltpu.make_async_copy(near_far, near, arrived)
    fetch_near.start()
    last = own + 2 * H

    def joined(block):
        parts = [block[slices + r : slices + r + 1, :].astype(jnp.float32) for r in range(9)]
        return jnp.concatenate([parts[r] + parts[r + 1] + parts[r + 2] for r in (0, 3, 6)], axis=0)

    def copy_along(slot):
        for r in range(3):
            along[slot, :, r * 128 : (r + 1) * 128] = jnp.broadcast_to(across[slot, r : r + 1], (128, CS)).T

    for slot in range(last):
        if slot < H:
            a = slot * CS
            block = low[:slices, a : a + CS]
            across[slot] = joined(low[:, a : a + CS])
        elif slot < H + own:
            block = sk[:, (slot - H) * CS : (slot - H + 1) * CS]
        else:
            a = (slot - H - own) * CS
            block = high[:slices, a : a + CS]
            across[slot] = joined(high[:, a : a + CS])
        cols[slot] = block
        acc[slot] = jnp.zeros((slices, CS), jnp.float32)
    for c in range(own):
        across[c + H] = pos[c, :3]
    cols[last] = jnp.zeros((slices, CS), jnp.bfloat16)
    along[last] = jnp.zeros((CS, 384), jnp.float32)
    across[last] = jnp.zeros((3, CS), jnp.float32)
    for slot in range(H, H + 3):
        copy_along(slot)
    for slot in range(H + own, last):
        copy_along(slot)

    def tile(c, s, i=0, j=0, size=CS):
        squared = 1e-30
        for r in range(3):
            point = along[s, i : i + size, r * 128 : (r + 1) * 128]
            if size > 128:
                point = jnp.concatenate([point, point], axis=1)
            diff = point - across[c, r : r + 1, j : j + size]
            squared = squared + diff * diff
        dist = squared * lax.rsqrt(squared)
        return ((1.0 + RATE * dist) * jnp.exp2(dist * (-RATE * math.log2(math.e)))).astype(jnp.bfloat16)

    def product(x, t):
        return jnp.dot(x, t, preferred_element_type=jnp.float32)

    def product_t(x, t):
        return lax.dot_general(x, t, (((1,), (1,)), ((), ())), preferred_element_type=jnp.float32)

    fetch_near.wait()
    count = jnp.int32(UNROLL)
    for s in range(H):
        for d in range(s + 1, H + 1):
            todo[count] = (s - d + H) * SHIFT + s + H
            count = count + near[s, H - d]

    def close_products(c, buf):
        x = cols[c]
        t = held[buf + 1]
        ahead = product(cols[c + 1], t)
        acc[c] = acc[c] + (product(x, held[buf]) + ahead)
        acc[c + 1] = acc[c + 1] + product_t(x, t)

    def close_tiles(c, buf):
        held[buf, :half, :half] = tile(c, c, 0, 0, half)
        corner = tile(c, c, 0, half, half)
        held[buf, :half, half:] = corner
        held[buf, half:, :half] = corner.T
        held[buf, half:, half:] = tile(c, c, half, half, half)
        held[buf + 1] = tile(c, c + 1)

    def close_step(i, count):
        c = i * 2 + H
        for u in range(2):
            close_products(c - 2 + u, 2 * u)
        for u in range(2):
            for d in range(2, H + 1):
                todo[count] = (c + u) * SHIFT + c + u + d
                count = count + near[c + u - H, H + d]
            copy_along(c + u + 3)
            close_tiles(c + u, 2 * u)
        return count

    held[...] = jnp.zeros(held.shape, jnp.bfloat16)
    count = lax.fori_loop(0, own // 2, close_step, count)
    for u in range(2):
        close_products(H + own - 2 + u, 2 * u)
    for slot in range(H):
        copy_along(slot)
    for i in range(UNROLL):
        todo[i] = last * (SHIFT + 1)
        todo[count + i] = last * (SHIFT + 1)

    def far_products(i):
        for u in range(UNROLL):
            code = todo[i * UNROLL + u]
            c, s = code // SHIFT, code % SHIFT
            t = held[u]
            acc[c] = acc[c] + product(cols[s], t)
            acc[s] = acc[s] + product_t(cols[c], t)

    def far_step(i, carry):
        far_products(i - 1)
        for u in range(UNROLL):
            code = todo[i * UNROLL + u]
            held[u] = tile(code // SHIFT, code % SHIFT)
        return carry

    steps = (count + UNROLL - 1) // UNROLL
    lax.fori_loop(1, steps, far_step, 0)
    far_products(steps - 1)

    per = own // rounded.shape[0]
    for c in range(own):
        value = acc[c + H] * (8.0 / CS) + NUGGET * cols[c + H].astype(jnp.float32)
        image[:, c * CS : (c + 1) * CS] = value
        rounded[c // per, :, (c % per) * CS : (c % per + 1) * CS] = value.astype(jnp.bfloat16)


def near_field(pos, sk, low, high, near, shares):
    slices, rows = sk.shape
    slots = rows // CS + 2 * H + 1
    whole = pl.BlockSpec(memory_space=pltpu.VMEM)
    far = pl.BlockSpec(memory_space=pltpu.HBM)
    return pl.pallas_call(
        near_field_kernel,
        out_shape=(
            jax.ShapeDtypeStruct((slices, rows), jnp.float32),
            jax.ShapeDtypeStruct((shares, slices, rows // shares), jnp.bfloat16),
        ),
        in_specs=[whole, whole, whole, whole, far],
        out_specs=(whole, whole),
        scratch_shapes=[
            pltpu.SMEM(near.shape, jnp.int32),
            pltpu.VMEM((slots, 3, CS), jnp.float32),
            pltpu.VMEM((slots, CS, 3 * 128), jnp.float32),
            pltpu.VMEM((slots, slices, CS), jnp.bfloat16),
            pltpu.VMEM((slots, slices, CS), jnp.float32),
            pltpu.VMEM((max(UNROLL, 4), CS, CS), jnp.bfloat16),
            pltpu.SMEM((slots * H + 4 * UNROLL,), jnp.int32),
            pltpu.SemaphoreType.DMA,
        ],
        compiler_params=pltpu.CompilerParams(vmem_limit_bytes=36 * MIB),
        name="near_field",
    )(pos, sk, low, high, near)


def gram_kernel(points, out, *, scale):
    whole = points[...].reshape(-1, points.shape[-1])
    half = whole.shape[0] // 2
    part = half // 2
    product = lax.dot_general(whole, whole, (((1,), (1,)), ((), ())), preferred_element_type=jnp.float32) * scale
    lane = lax.broadcasted_iota(jnp.int32, (part, half), 1)
    corner = pltpu.roll(product[half + part :, half:], part, 1)
    mixed = jnp.where(lane < part, corner, product[part:half, :half])
    for i in range(out.shape[0]):
        out[i, :part] = product[:part, :half]
        out[i, part : 2 * part] = product[:part, half:]
        out[i, 2 * part : 3 * part] = product[part:half, half:]
        out[i, 3 * part : 4 * part] = product[half : half + part, half:]
        out[i, 4 * part :] = mixed


def partial_gram(points, scale, copies):
    half = points.shape[0] * points.shape[1] // 2
    return pl.pallas_call(
        lambda points, out: gram_kernel(points, out, scale=scale),
        out_shape=jax.ShapeDtypeStruct((copies, 5 * half // 2, half), jnp.float32),
        compiler_params=pltpu.CompilerParams(vmem_limit_bytes=32 * MIB),
        name="partial_gram",
    )(points)


def pieces(value):
    high = value.astype(jnp.bfloat16)
    rest = value - high.astype(jnp.float32)
    mid = rest.astype(jnp.bfloat16)
    low = (rest - mid.astype(jnp.float32)).astype(jnp.bfloat16)
    return high, mid, low


def cholesky_kernel(place, grams, *refs):
    outs, (work, upper) = refs[:-2], refs[-2:]
    mats = len(outs)
    half = work.shape[1] // 2
    part = half // 2
    n = 2 * half
    for m in range(mats):
        for block in range(5):
            value = grams[m, block * part : (block + 1) * part]
            if block == 0:
                work[m, :part, :half] = value
            elif block == 1:
                work[m, :part, half:] = value
            elif block == 2:
                work[m, part:half, half:] = value
            elif block == 3:
                work[m, half : half + part, half:] = value
            else:
                work[m, part:half, :half] = value
                work[m, half + part :, half:] = pltpu.roll(value, part, 1)
    for m in range(mats):
        upper[m, half:, :half] = jnp.zeros((half, half), jnp.float32)
    rowid = lax.broadcasted_iota(jnp.int32, (8, 128), 0)
    spread = lambda row: jnp.broadcast_to(row, (8, 128))
    blank = upper[0, half : half + 8, :half]
    for j0 in range(0, n, PANEL):
        lane0 = 0 if j0 < half else half
        width = (n - lane0) // 128
        rows, cols, scale = [], [], []
        for m in range(mats):
            block = work[m, j0 : j0 + PANEL, lane0:]
            rows.append(
                [[block[8 * h : 8 * h + 8, 128 * w : 128 * w + 128] for w in range(width)] for h in range(2)]
            )
            at = j0 - lane0
            cols.append(
                [[spread(block[8 * h : 8 * h + 8, at + c : at + c + 1]) + blank for h in range(2)] for c in range(PANEL)]
            )
            scale.append([jnp.zeros((8, 128), jnp.float32) for h in range(2)])
        for q in range(PANEL):
            hq, r = q // 8, q % 8
            for m in range(mats):
                inv = lax.rsqrt(spread(cols[m][q][hq][r : r + 1, :]))
                scale[m][hq] = jnp.where(rowid == r, inv, scale[m][hq])
                inv2 = inv * inv
                factor = [None, None]
                for h in range(hq, 2):
                    f = cols[m][q][h] * inv2
                    factor[h] = jnp.where(rowid > r, f, 0.0) if h == hq else f
                for c in range(q + 1, PANEL):
                    row = spread(cols[m][c][hq][r : r + 1, :])
                    for h in range(hq, 2):
                        cols[m][c][h] = cols[m][c][h] - factor[h] * row
                for w in range(width):
                    row = spread(rows[m][hq][w][r : r + 1, :])
                    for h in range(hq, 2):
                        rows[m][h][w] = rows[m][h][w] - factor[h] * row
        start = j0 + PANEL
        for m in range(mats):
            done = jnp.concatenate(
                [
                    jnp.concatenate([rows[m][h][w] * scale[m][h] for w in range(width)], axis=1)
                    for h in range(2)
                ],
                axis=0,
            )
            upper[m, j0 : j0 + PANEL, lane0:] = done
            if start < n:
                high, mid, low = pieces(done)
                left = jnp.concatenate([high, high, mid, high, mid, low], axis=0)
                right = jnp.concatenate([high, mid, high, low, mid, high], axis=0)
                skip = (0 if start < half else half) - lane0
                product = lax.dot_general(
                    left[:, skip:], right[:, skip:], (((0,), (0,)), ((), ())), preferred_element_type=jnp.float32
                )
                if start < half:
                    work[m, start:half, :] = work[m, start:half, :] - product[start:half, :]
                    work[m, half:, half:] = work[m, half:, half:] - product[half:, half:]
                else:
                    work[m, start:, half:] = work[m, start:, half:] - product[start - half :, :]
    wide = outs[0].shape[0]
    begin = pl.multiple_of(place[0] * wide, wide)
    i = lax.broadcasted_iota(jnp.int32, (wide, n), 0) + begin
    j = lax.broadcasted_iota(jnp.int32, (wide, n), 1)
    for m, out in enumerate(outs):
        out[...] = jnp.where(j >= i, upper[m, pl.ds(begin, wide), :], 0.0)


def cholesky(place, grams, wide):
    mats, half = grams.shape[0], grams.shape[2]
    whole = pl.BlockSpec(memory_space=pltpu.VMEM)
    return pl.pallas_call(
        cholesky_kernel,
        out_shape=(jax.ShapeDtypeStruct((wide, 2 * half), jnp.float32),) * mats,
        in_specs=[pl.BlockSpec(memory_space=pltpu.SMEM), whole],
        out_specs=(whole,) * mats,
        scratch_shapes=[pltpu.VMEM((mats, 2 * half, 2 * half), jnp.float32)] * 2,
        compiler_params=pltpu.CompilerParams(vmem_limit_bytes=32 * MIB),
        name="cholesky",
    )(place, grams)


def edge(positions, sketch):
    high = lax.reduce_precision(positions, 8, 7)
    rest = positions - high
    mid = lax.reduce_precision(rest, 8, 7)
    parts = jnp.stack([high, mid, rest - mid], axis=1).reshape(9, -1).astype(jnp.bfloat16)
    return jnp.concatenate([sketch, jnp.pad(parts, ((0, 7), (0, 0)))], axis=0)


def on_device(positions, sketch, near):
    slices, rows = sketch.shape
    margin = H * CS
    clus = ("tree", "child")
    count = lax.axis_size(clus)
    shares = lax.axis_size("sk")
    forward = [(i, i + 1) for i in range(count - 1)]
    backward = [(i + 1, i) for i in range(count - 1)]
    low = lax.ppermute(edge(positions[:, -margin:], sketch[:, -margin:]), clus, forward)
    high = lax.ppermute(edge(positions[:, :margin], sketch[:, :margin]), clus, backward)
    by_cluster = jnp.pad(positions, ((0, 1), (0, 0))).reshape(4, -1, CS).transpose(1, 0, 2)
    image, rounded = near_field(by_cluster, sketch, low, high, near, shares)
    traded = lax.all_to_all(rounded, "sk", split_axis=0, concat_axis=0, tiled=True)
    shared = partial_gram(traded, 1.0 / rows, shares)
    parts = lax.all_to_all(shared, "sk", split_axis=0, concat_axis=0, tiled=True)
    node = jnp.sum(parts, axis=0)
    sibling = lambda value, d: lax.ppermute(value, "child", [(i, i ^ d) for i in range(FAMILY)])
    pair = (node + sibling(node, 1)) * 0.5
    group = (pair + sibling(pair, 2)) * 0.5
    place = lax.axis_index("sk").astype(jnp.int32).reshape(1)
    factors = cholesky(place, jnp.stack([node, pair, group]), slices)
    return (image, *(factor.T for factor in factors))


def solution(mesh):
    clusters, shares = mesh.devices.shape
    split = Mesh(mesh.devices.reshape(clusters // FAMILY, FAMILY, shares), ("tree", "child", "sk"))
    clus = ("tree", "child")
    return jax.shard_map(
        on_device,
        mesh=split,
        in_specs=(P(None, clus), P("sk", clus), P(clus, None)),
        out_specs=(P("sk", clus), P(clus, "sk"), P(clus, "sk"), P(clus, "sk")),
        check_vma=False,
    )
```
